512 devices in a mesh: head: 32 (over x, y_lo, core), ctx: 16 (over z, y_hi).
Axes of the slice: x: 4, y: 8 (y_hi: 2, y_lo: 4; y = y_hi * 4 + y_lo), z: 8, core: 2. Of those that a mesh axis runs over, the one named last changes fastest.
Arguments:
- queries: bfloat16 [8192, 8192], P(('head', 'ctx')), may hold values from -6 to 6
- keys: bfloat16 [8192, 8192], P(('head', 'ctx')), may hold values from -6 to 6
- values: bfloat16 [8192, 8192], P(('head', 'ctx')), may hold values from -6 to 6
- doc_lengths: int32 [8], replicated, may hold values from 1 to 4096, 8192 in all
- slab_owner: int32 [512], replicated, may hold values from 0 to 15, as said below
Outputs:
- context: bfloat16 [8192, 8192], P('ctx', 'head')
The draws below stay inside these ranges and needn't reach their ends.
Inputs may be any that keep to these rules, and one draw needn't show every extreme that they name: `doc_lengths`: the 8 lengths sum to 8192 and the longest is exactly 4096. `slab_owner`: slab h * 16 + c lies on the device of head index h and ctx index c. Every owner receives exactly 32 slabs. Of the 32 slabs that share one ctx index, at most 4 go to one owner, and for every ctx index some owner receives exactly 4 of them.
All inputs are finite; a program needn't handle non-finite values.
Results may differ from the reference program's by a relative error of at most 0.0065.
Values may be sent and summed in bfloat16 or wider, within the bound.
No kernel may reach another device: no remote copies, remote signals or barrier semaphores. Data moves between devices by JAX's collectives and lax.ppermute only.
A program may use at most 64 MiB of HBM per device.

```python
import math
import jax
import jax.numpy as jnp
import numpy as np
from jax import lax

HEADS = 64
DH = 128
TOK_DEV = 512
DOCS = 8
TOKENS = 8192
SLAB = 16
SLABS = 512
CAP = 4
DOC_MOST = 4096
N_HEAD = 32
N_CTX = 16


def draw_queries(key, part):
    own_key = jax.random.fold_in(key, 21)
    field = jnp.clip(jax.random.normal(own_key, (TOKENS, HEADS * DH), jnp.float32), -6.0, 6.0)
    return field.astype(jnp.bfloat16)


def draw_keys(key, part):
    own_key = jax.random.fold_in(key, 22)
    field = jnp.clip(jax.random.normal(own_key, (TOKENS, HEADS * DH), jnp.float32), -6.0, 6.0)
    return field.astype(jnp.bfloat16)


def draw_slab_owner(key, part):
    key = jax.random.fold_in(key, 23)
    key_columns, key_order, key_shift = jax.random.split(key, 3)
    column_base = jax.random.permutation(key_columns, N_CTX)
    head_order = jax.random.permutation(key_order, N_HEAD)
    rotation = jax.random.randint(key_shift, (), 0, N_CTX)
    head_rank = jnp.arange(N_HEAD)
    offsets = jnp.where(head_rank < CAP, 0, 1 + (head_rank - CAP) % (N_CTX - 1))
    head_offset = (offsets[head_order] + rotation) % N_CTX
    owners = (column_base[None, :] + head_offset[:, None]) % N_CTX
    return owners.reshape(-1).astype(jnp.int32)


def level_of(rng, dims, pieces, smallest, top_value):
    level, own = 1.0, jax.random.fold_in(rng, 6)
    for position, shards_of in pieces:
        steps = jnp.exp(jax.random.uniform(jax.random.fold_in(own, position), (shards_of,), jnp.float32, smallest / len(pieces), top_value / len(pieces)))
        level = level * jnp.repeat(steps, dims[position] // shards_of).reshape([-1 if axis == position else 1 for axis in range(len(dims))])
    return level


def split_up(number_of, total, bound, slope):
    loads = [(1 << 20) // math.isqrt(rank ** slope) + 1 for rank in range(2, number_of + 1)]
    spare, holding = total - bound - (number_of - 1), [1] * (number_of - 1)
    while spare > 0:
        free = [i for i in range(number_of - 1) if holding[i] < bound]
        whole, remaining = sum([loads[i] for i in free]), spare
        for i in free:
            more = min(bound - holding[i], max(1, remaining * loads[i] // whole), spare)
            holding[i] = holding[i] + more
            spare = spare - more
    return np.array([bound] + holding)


def uneven_parts(key, number_of, total, most, slope):
    if number_of == 2:
        one = jax.random.randint(key, (), max(1, total - most), min(most, total - 1) + 1)
        return jnp.stack([one, total - one])
    sizes = jnp.asarray(split_up(number_of, total, most, slope), jnp.int32)
    pairs = (number_of - 1) // 2
    giver, sink = sizes[1:1 + 2 * pairs:2], sizes[2:2 + 2 * pairs:2]
    slack = jnp.minimum(giver - 1, most - sink)
    shifted = jax.random.randint(jax.random.fold_in(key, 1), (pairs,), 0, 1 << 20) % (slack + 1)
    sizes = sizes.at[1:1 + 2 * pairs:2].set(giver - shifted).at[2:2 + 2 * pairs:2].set(sink + shifted)
    return sizes[jax.random.permutation(jax.random.fold_in(key, 2), number_of)]


def normal_values(stream_key, extent, scale, reach, cuts=(), kind=jnp.bfloat16):
    result = jax.random.normal(stream_key, extent, jnp.float32) * scale
    if len(cuts) > 0:
        result = level_of(stream_key, extent, cuts, -0.22, 0.18) * result
    return jnp.clip(result, min=-reach, max=reach).astype(kind)


def setup_inputs(seed: int = 0) -> dict:
    seeds = jax.random.split(jax.random.key(seed), 6)
    return {
        "queries": draw_queries(jax.random.fold_in(seeds[5], 71), 0),
        "keys": draw_keys(jax.random.fold_in(seeds[5], 71), 0),
        "values": normal_values(seeds[2], (TOKENS, HEADS * DH), 1.0, 6.0, ((0, 512),)),
        "doc_lengths": uneven_parts(seeds[3], DOCS, TOKENS, DOC_MOST, 2).astype(jnp.int32),
        "slab_owner": draw_slab_owner(jax.random.fold_in(seeds[5], 71), 0),
    }


def reference(queries, keys, values, doc_lengths, slab_owner):
    token_index = jnp.arange(TOKENS, dtype=jnp.int32)
    doc_ends = jnp.cumsum(doc_lengths).astype(jnp.int32)[:-1]
    documents = jnp.sum((token_index[:, None] >= doc_ends[None, :]).astype(jnp.int32), axis=1).astype(jnp.int32)

    def split_heads(matrix):
        return matrix.astype(jnp.float32).reshape(TOKENS, HEADS // 8, 8, DH).transpose(1, 2, 0, 3)

    query_heads = split_heads(queries)
    key_heads = split_heads(keys)
    value_heads = split_heads(values)
    block_count = TOKENS // TOK_DEV

    def one_group(head_group):
        query_group, key_group, value_group = head_group

        def one_block(block_index):
            first_row = (block_index * TOK_DEV).astype(jnp.int32)
            query_rows = lax.dynamic_slice_in_dim(query_group, first_row, TOK_DEV, 1)
            query_pos = lax.dynamic_slice_in_dim(token_index, first_row, TOK_DEV)
            query_doc = lax.dynamic_slice_in_dim(documents, first_row, TOK_DEV)
            allowed = (query_doc[:, None] == documents[None, :]) & (token_index[None, :] <= query_pos[:, None])
            scores = jnp.einsum("hqd,hkd->hqk", query_rows, key_group) * (DH ** -0.5)
            scores = jnp.where(allowed[None], scores, -1e30)
            highest = jnp.max(scores, axis=2, keepdims=True)
            weights = jnp.where(allowed[None], jnp.exp(scores - highest), 0.0)
            denominator = jnp.sum(weights, axis=2, keepdims=True)
            rounded = lax.optimization_barrier(weights.astype(jnp.bfloat16)).astype(jnp.float32)
            weighted = jnp.einsum("hqk,hkd->hqd", rounded, value_group)
            return weighted / denominator

        outputs = lax.map(one_block, jnp.arange(block_count, dtype=jnp.int32))
        return outputs.transpose(1, 0, 2, 3).reshape(8, TOKENS, DH)

    attended = lax.map(one_group, (query_heads, key_heads, value_heads))
    attended = attended.reshape(HEADS, TOKENS, DH).transpose(1, 0, 2).reshape(TOKENS, HEADS * DH).astype(jnp.bfloat16)
    slab_index = jnp.arange(SLABS, dtype=jnp.int32)
    same_owner = slab_owner[:, None] == slab_owner[None, :]
    owner_rank = jnp.sum((same_owner & (slab_index[None, :] < slab_index[:, None])).astype(jnp.int32), axis=1).astype(jnp.int32)
    new_slab = (slab_owner * N_HEAD + owner_rank).astype(jnp.int32)
    portions = attended.reshape(SLABS, SLAB, HEADS * DH)
    context = jnp.zeros_like(portions).at[new_slab].set(portions)
    return context.reshape(TOKENS, HEADS * DH)
```

```python
import jax
import jax.numpy as jnp
from jax import lax
from jax.experimental import pallas as pl
from jax.experimental.pallas import tpu as pltpu
from jax.sharding import Mesh, PartitionSpec as P

DH = 128
SLAB = 16
TOKENS = 8192
HEADS = 64
TQ = 128
BK = 512
ROWS = 1024
SLABS_HERE = ROWS // SLAB
FOLD = DH ** (-0.5) * 1.4426950408889634
AXES = ("x", "yl", "core", "zh", "zl", "yh")
HEAD_AXES = ("zh", "yl", "zl", "yh")


def split_kernel(q_ref, k_ref, v_ref, out_ref):
    for n in range(HEADS):
        cols = slice(n * DH, (n + 1) * DH)
        out_ref[n, 0:16, :] = q_ref[:, cols]
        out_ref[n, 16:32, :] = k_ref[:, cols]
        out_ref[n, 32:48, :] = v_ref[:, cols]


def split_heads(queries, keys, values):
    vmem = pl.BlockSpec(memory_space=pltpu.VMEM)
    return pl.pallas_call(
        split_kernel,
        out_shape=jax.ShapeDtypeStruct((HEADS, 48, DH), jnp.bfloat16),
        in_specs=[vmem, vmem, vmem],
        out_specs=vmem,
        name="split_heads",
    )(queries, keys, values)


def doc_start(positions, starts):
    first = jnp.zeros_like(positions)
    for start in starts:
        first = jnp.where(positions >= start, start, first)
    return first


def attend_kernel(slab_ref, dst_ref, start_ref, all_ref, out_ref, q_s, k_s, v_s, sem_q, sem_k, sem_v):
    def fetch_query(r, carry):
        j = slab_ref[r]
        h, c = j >> 4, j & 15
        shard = (h >> 3) * 2 + (h & 1)
        pltpu.make_async_copy(
            all_ref.at[shard, c >> 2, (h >> 1) & 3, c & 3, pl.ds(0, SLAB), :],
            q_s.at[pl.ds(pl.multiple_of(r * SLAB, SLAB), SLAB), :],
            sem_q,
        ).start()
        return carry

    lax.fori_loop(0, SLABS_HERE, fetch_query, 0)
    for x in range(4):
        for core in range(2):
            for yl in range(4):
                h = x * 8 + yl * 2 + core
                for buf, lo, sem in ((k_s, 16, sem_k), (v_s, 32, sem_v)):
                    pltpu.make_async_copy(
                        all_ref.at[x * 2 + core, :, yl, :, pl.ds(lo, SLAB), :],
                        buf.at[h],
                        sem,
                    ).start()
    pltpu.make_async_copy(q_s, q_s, sem_q).wait()
    pltpu.make_async_copy(k_s, k_s, sem_k).wait()
    pltpu.make_async_copy(v_s, v_s, sem_v).wait()
    starts = [start_ref[i] for i in range(8)]
    per_tile = TQ // SLAB
    blocks = BK // 256

    def tile(t, carry):
        q = q_s[pl.ds(pl.multiple_of(t * TQ, TQ), TQ), :]
        slabs = [slab_ref[t * per_tile + i] for i in range(per_tile)]
        row = lax.broadcasted_iota(jnp.int32, (SLAB, DH), 0)
        pos = jnp.concatenate([row + j * SLAB for j in slabs], axis=0)
        low = doc_start(pos, starts)
        first_pos = slabs[0] * SLAB
        last_pos = slabs[-1] * SLAB + SLAB - 1
        low_first = doc_start(first_pos, starts)
        low_last = doc_start(last_pos, starts)
        begin = low_first // BK
        end = last_pos // BK + 1
        full_begin = (low_last + BK - 1) // BK
        full_end = jnp.maximum((first_pos + 1) // BK, full_begin)
        full_begin = jnp.minimum(full_begin, end)
        full_end = jnp.minimum(full_end, end)

        def block(masked):
            def body(i, state):
                high, denom, acc = state
                k = k_s[pl.ds(i * blocks, blocks)].reshape(BK, DH)
                v = v_s[pl.ds(i * blocks, blocks)].reshape(BK, DH)
                s = lax.dot_general(
                    q, k, (((1,), (1,)), ((), ())), preferred_element_type=jnp.float32
                )
                if masked:
                    lane = lax.broadcasted_iota(jnp.int32, (TQ, DH), 1) + i * BK
                    parts = []
                    for m in range(BK // DH):
                        u = lane + m * DH
                        ok = (u >= low) & (u <= pos)
                        parts.append(jnp.where(ok, s[:, m * DH:(m + 1) * DH], -1e30))
                else:
                    parts = [s[:, m * DH:(m + 1) * DH] for m in range(BK // DH)]
                top = parts[0]
                for part in parts[1:]:
                    top = jnp.maximum(top, part)
                top = jnp.max(top, axis=1, keepdims=True) * FOLD
                new_high = jnp.maximum(high, jnp.broadcast_to(top, (TQ, DH)))
                scale = jnp.exp2(high - new_high)
                weights = [jnp.exp2(part * FOLD - new_high) for part in parts]
                denom = denom * scale
                for w in weights:
                    denom = denom + w
                p = jnp.concatenate([w.astype(jnp.bfloat16) for w in weights], axis=1)
                acc = acc * scale + jnp.dot(p, v, preferred_element_type=jnp.float32)
                return new_high, denom, acc

            return body

        state = (
            jnp.full((TQ, DH), -1e30, jnp.float32),
            jnp.zeros((TQ, DH), jnp.float32),
            jnp.zeros((TQ, DH), jnp.float32),
        )
        state = lax.fori_loop(begin, full_begin, block(True), state)
        state = lax.fori_loop(full_begin, full_end, block(False), state)
        state = lax.fori_loop(full_end, end, block(True), state)
        high, denom, acc = state
        result = (acc / jnp.sum(denom, axis=1, keepdims=True)).astype(jnp.bfloat16)
        for i in range(per_tile):
            to = pl.multiple_of(dst_ref[t * per_tile + i], SLAB)
            out_ref[pl.ds(to, SLAB), :] = result[i * SLAB:(i + 1) * SLAB]
        return carry

    lax.fori_loop(0, ROWS // TQ, tile, 0)


def attend(slabs, dst, starts, gathered):
    smem = pl.BlockSpec(memory_space=pltpu.SMEM)
    return pl.pallas_call(
        attend_kernel,
        out_shape=jax.ShapeDtypeStruct((ROWS, DH), jnp.bfloat16),
        in_specs=[smem, smem, smem, pl.BlockSpec(memory_space=pl.ANY)],
        out_specs=pl.BlockSpec(memory_space=pltpu.VMEM),
        scratch_shapes=[
            pltpu.VMEM((ROWS, DH), jnp.bfloat16),
            pltpu.VMEM((32, 4, 4, SLAB, DH), jnp.bfloat16),
            pltpu.VMEM((32, 4, 4, SLAB, DH), jnp.bfloat16),
            pltpu.SemaphoreType.DMA,
            pltpu.SemaphoreType.DMA,
            pltpu.SemaphoreType.DMA,
        ],
        compiler_params=pltpu.CompilerParams(vmem_limit_bytes=32 * 1024 * 1024),
        cost_estimate=pl.CostEstimate(flops=2 * 10**9, bytes_accessed=8 * 2**20, transcendentals=2 * 10**6),
        name="attend",
    )(slabs, dst, starts, gathered)


def tables(doc_lengths, slab_owner):
    part = lax.axis_index("x") * 2 + lax.axis_index("core")
    yh = lax.axis_index("yh")
    n = slab_owner.shape[0]
    index = jnp.arange(n, dtype=jnp.int32)
    mine = (slab_owner >> 1) == part
    before = jnp.sum((mine[None, :] & (index[None, :] < index[:, None])).astype(jnp.int32), axis=1)
    here = jnp.arange(SLABS_HERE, dtype=jnp.int32)
    hit = mine[None, :] & (before[None, :] == here[:, None])
    slabs = jnp.sum(jnp.where(hit, index[None, :], 0), axis=1)
    low_owner = jnp.sum(jnp.where(hit, slab_owner[None, :] & 1, 0), axis=1)
    rank = jnp.sum(
        ((low_owner[None, :] == low_owner[:, None]) & (here[None, :] < here[:, None])).astype(jnp.int32),
        axis=1,
    )
    dst = (low_owner ^ yh) * 512 + rank * SLAB
    earlier = jnp.arange(8)[None, :] < jnp.arange(8)[:, None]
    starts = jnp.sum(jnp.where(earlier, doc_lengths[None, :], 0), axis=1)
    return slabs, dst, starts


def to_owner(swap):
    route = []
    for x in range(4):
        for core in range(2):
            for z in range(8):
                for yh in range(2):
                    source = ((x * 2 + core) * 8 + z) * 2 + yh
                    target = (z * 8 + (x * 2 + core)) * 2 + (yh ^ swap)
                    route.append((source, target))
    return route


def per_device(queries, keys, values, doc_lengths, slab_owner):
    slabs, dst, starts = tables(doc_lengths, slab_owner)
    parted = split_heads(queries, keys, values)
    landed = lax.all_to_all(parted, HEAD_AXES, split_axis=0, concat_axis=0, tiled=True)
    gathered = lax.all_gather(landed, ("x", "core"), axis=0, tiled=False)
    gathered = gathered.reshape(8, 4, 4, 4, 48, DH)
    attended = attend(slabs, dst, starts, gathered)
    moved = ("x", "core", "zh", "zl", "yh")
    same = lax.ppermute(attended[:512], moved, to_owner(0))
    other = lax.ppermute(attended[512:], moved, to_owner(1))
    first = lax.axis_index("yh") == 0
    return jnp.concatenate(
        [jnp.where(first, same, other), jnp.where(first, other, same)], axis=1
    )


def solution(mesh):
    fine = Mesh(mesh.devices.reshape(4, 4, 2, 4, 2, 2), AXES)
    rows = P(AXES, None)
    return jax.shard_map(
        per_device,
        mesh=fine,
        in_specs=(rows, rows, rows, P(), P()),
        out_specs=P(("zh", "zl", "yh"), ("x", "yl", "core")),
        check_vma=False,
    )
```

```python
import jax
import jax.numpy as jnp
from jax import lax
from jax.experimental import pallas as pl
from jax.experimental.pallas import tpu as pltpu
from jax.sharding import Mesh, PartitionSpec as P

DH = 128
SLAB = 16
TOKENS = 8192
HEADS = 64
TQ = 128
BK = 2048
ROWS = 1024
SLABS_HERE = ROWS // SLAB
FOLD = DH ** (-0.5) * 1.4426950408889634
AXES = ("x", "yl", "core", "zh", "zl", "yh")
HEAD_AXES = ("zh", "yl", "zl", "yh")


def split_kernel(q_ref, k_ref, v_ref, out_ref):
    for n in range(HEADS):
        cols = slice(n * DH, (n + 1) * DH)
        out_ref[n, 0:16, :] = q_ref[:, cols]
        out_ref[n, 16:32, :] = k_ref[:, cols]
        out_ref[n, 32:48, :] = v_ref[:, cols]


def split_heads(queries, keys, values):
    vmem = pl.BlockSpec(memory_space=pltpu.VMEM)
    return pl.pallas_call(
        split_kernel,
        out_shape=jax.ShapeDtypeStruct((HEADS, 48, DH), jnp.bfloat16),
        in_specs=[vmem, vmem, vmem],
        out_specs=vmem,
        name="split_heads",
    )(queries, keys, values)


def doc_start(positions, starts):
    first = jnp.zeros_like(positions)
    for start in starts:
        first = jnp.where(positions >= start, start, first)
    return first


def attend_kernel(slab_ref, dst_ref, start_ref, home_ref, *refs):
    shards, (out_ref, q_s, k_s, v_s, sem_q, sem_k, sem_v) = refs[:8], refs[8:]
    for i, shard in enumerate(shards):
        for yl in range(4):
            h = home_ref[i] + yl * 2
            for buf, lo, sem in ((q_s, 0, sem_q), (k_s, 16, sem_k), (v_s, 32, sem_v)):
                pltpu.make_async_copy(
                    shard.at[:, yl, :, pl.ds(lo, SLAB), :], buf.at[h], sem
                ).start()
    pltpu.make_async_copy(q_s, q_s, sem_q).wait()
    pltpu.make_async_copy(k_s, k_s, sem_k).wait()
    pltpu.make_async_copy(v_s, v_s, sem_v).wait()
    starts = [start_ref[i] for i in range(8)]
    per_tile = TQ // SLAB
    blocks = BK // 256

    def tile(t, carry):
        slabs = [slab_ref[t * per_tile + i] for i in range(per_tile)]
        q = jnp.concatenate([q_s[j >> 4, (j >> 2) & 3, j & 3] for j in slabs], axis=0)
        row = lax.broadcasted_iota(jnp.int32, (SLAB, DH), 0)
        pos = jnp.concatenate([row + j * SLAB for j in slabs], axis=0)
        low = doc_start(pos, starts)
        first_pos = slabs[0] * SLAB
        last_pos = slabs[-1] * SLAB + SLAB - 1
        low_first = doc_start(first_pos, starts)
        low_last = doc_start(last_pos, starts)
        begin = low_first >> 8
        count = (last_pos + 1 - begin * 256 + BK - 1) // BK
        begin = jnp.minimum(begin, 32 - count * blocks)
        base = begin * 256
        full_begin = jnp.minimum((jnp.maximum(low_last - base, 0) + BK - 1) // BK, count)
        full_end = jnp.clip((first_pos + 1 - base) // BK, full_begin, count)

        def block(masked):
            def body(i, state):
                high, denom, acc = state
                k = k_s[pl.ds(begin + i * blocks, blocks)].reshape(BK, DH)
                v = v_s[pl.ds(begin + i * blocks, blocks)].reshape(BK, DH)
                s = lax.dot_general(
                    q, k, (((1,), (1,)), ((), ())), preferred_element_type=jnp.float32
                )
                if masked:
                    lane = lax.broadcasted_iota(jnp.int32, (TQ, DH), 1) + (base + i * BK)
                    parts = []
                    for m in range(BK // DH):
                        u = lane + m * DH
                        ok = (u >= low) & (u <= pos)
                        parts.append(jnp.where(ok, s[:, m * DH:(m + 1) * DH], -1e30))
                else:
                    parts = [s[:, m * DH:(m + 1) * DH] for m in range(BK // DH)]
                top = parts[0]
                for part in parts[1:]:
                    top = jnp.maximum(top, part)
                top = jnp.max(top, axis=1, keepdims=True) * FOLD
                new_high = jnp.maximum(high, jnp.broadcast_to(top, (TQ, DH)))
                scale = jnp.exp2(high - new_high)
                weights = [jnp.exp2(part * FOLD - new_high) for part in parts]
                denom = denom * scale
                for w in weights:
                    denom = denom + w
                p = jnp.concatenate([w.astype(jnp.bfloat16) for w in weights], axis=1)
                acc = acc * scale + jnp.dot(p, v, preferred_element_type=jnp.float32)
                return new_high, denom, acc

            return body

        state = (
            jnp.full((TQ, DH), -1e30, jnp.float32),
            jnp.zeros((TQ, DH), jnp.float32),
            jnp.zeros((TQ, DH), jnp.float32),
        )
        state = lax.fori_loop(0, count, block(True), state)
        high, denom, acc = state
        result = (acc / jnp.sum(denom, axis=1, keepdims=True)).astype(jnp.bfloat16)
        for i in range(per_tile):
            to = pl.multiple_of(dst_ref[t * per_tile + i], SLAB)
            out_ref[pl.ds(to, SLAB), :] = result[i * SLAB:(i + 1) * SLAB]
        return carry

    lax.fori_loop(0, ROWS // TQ, tile, 0)


def attend(slabs, dst, starts, homes, shards):
    smem = pl.BlockSpec(memory_space=pltpu.SMEM)
    shards = [shard.reshape(4, 4, 4, 48, DH) for shard in shards]
    whole = pltpu.VMEM((32, 4, 4, SLAB, DH), jnp.bfloat16)
    return pl.pallas_call(
        attend_kernel,
        out_shape=jax.ShapeDtypeStruct((ROWS, DH), jnp.bfloat16),
        in_specs=[smem] * 4 + [pl.BlockSpec(memory_space=pl.ANY)] * 8,
        out_specs=pl.BlockSpec(memory_space=pltpu.VMEM),
        scratch_shapes=[whole, whole, whole] + [pltpu.SemaphoreType.DMA] * 3,
        compiler_params=pltpu.CompilerParams(vmem_limit_bytes=32 * 1024 * 1024),
        cost_estimate=pl.CostEstimate(
            flops=2 * 10**9, bytes_accessed=8 * 2**20, transcendentals=2 * 10**6
        ),
        name="attend",
    )(slabs, dst, starts, homes, *shards)


def tables(doc_lengths, slab_owner):
    part = lax.axis_index("x") * 2 + lax.axis_index("core")
    yh = lax.axis_index("yh")
    n = slab_owner.shape[0]
    index = jnp.arange(n, dtype=jnp.int32)
    mine = (slab_owner >> 1) == part
    before = jnp.sum((mine[None, :] & (index[None, :] < index[:, None])).astype(jnp.int32), axis=1)
    here = jnp.arange(SLABS_HERE, dtype=jnp.int32)
    hit = mine[None, :] & (before[None, :] == here[:, None])
    slabs = jnp.sum(jnp.where(hit, index[None, :], 0), axis=1)
    low_owner = jnp.sum(jnp.where(hit, slab_owner[None, :] & 1, 0), axis=1)
    rank = jnp.sum(
        ((low_owner[None, :] == low_owner[:, None]) & (here[None, :] < here[:, None])).astype(jnp.int32),
        axis=1,
    )
    dst = (low_owner ^ yh) * 512 + rank * SLAB
    earlier = jnp.arange(8)[None, :] < jnp.arange(8)[:, None]
    starts = jnp.sum(jnp.where(earlier, doc_lengths[None, :], 0), axis=1)
    return slabs, dst, starts


def to_owner(swap):
    route = []
    for x in range(4):
        for core in range(2):
            for z in range(8):
                for yh in range(2):
                    source = ((x * 2 + core) * 8 + z) * 2 + yh
                    target = (z * 8 + (x * 2 + core)) * 2 + (yh ^ swap)
                    route.append((source, target))
    return route


def row_route(turn):
    route = []
    for x in range(4):
        for core in range(2):
            to_x, to_core = turn(x, core)
            route.append((x * 2 + core, (to_x % 4) * 2 + to_core))
    return route


def gather_row(mine):
    row = ("x", "core")
    ring = row_route(lambda x, core: (x + 1 - 2 * core, core))
    crossed = row_route(lambda x, core: (x - 1 + 2 * core, 1 - core))
    swap = row_route(lambda x, core: (x, 1 - core))
    near = lax.ppermute(mine, row, ring)
    near_other = lax.ppermute(mine, row, crossed)
    other = lax.ppermute(mine, row, swap)
    far = lax.ppermute(near, row, ring)
    back = lax.ppermute(near, row, swap)
    back_other = lax.ppermute(near_other, row, swap)
    far_other = lax.ppermute(far, row, swap)
    x, core = lax.axis_index("x"), lax.axis_index("core")
    behind = x - 1 + 2 * core
    ahead = x + 1 - 2 * core
    homes = jnp.stack(
        [
            (at & 3) * 8 + c
            for at, c in (
                (x, core),
                (x, 1 - core),
                (behind, core),
                (behind, 1 - core),
                (x + 2, core),
                (ahead, 1 - core),
                (ahead, core),
                (x + 2, 1 - core),
            )
        ]
    )
    return (mine, other, near, near_other, far, back, back_other, far_other), homes


def per_device(queries, keys, values, doc_lengths, slab_owner):
    slabs, dst, starts = tables(doc_lengths, slab_owner)
    parted = split_heads(queries, keys, values)
    landed = lax.all_to_all(parted, HEAD_AXES, split_axis=0, concat_axis=0, tiled=True)
    shards, homes = gather_row(landed)
    attended = attend(slabs, dst, starts, homes, shards)
    moved = ("x", "core", "zh", "zl", "yh")
    same = lax.ppermute(attended[:512], moved, to_owner(0))
    other = lax.ppermute(attended[512:], moved, to_owner(1))
    first = lax.axis_index("yh") == 0
    return jnp.concatenate(
        [jnp.where(first, same, other), jnp.where(first, other, same)], axis=1
    )


def solution(mesh):
    fine = Mesh(mesh.devices.reshape(4, 4, 2, 4, 2, 2), AXES)
    rows = P(AXES, None)
    return jax.shard_map(
        per_device,
        mesh=fine,
        in_specs=(rows, rows, rows, P(), P()),
        out_specs=P(("zh", "zl", "yh"), ("x", "yl", "core")),
        check_vma=False,
    )
```

```python
import jax
import jax.numpy as jnp
from jax import lax
from jax.experimental import pallas as pl
from jax.experimental.pallas import tpu as pltpu
from jax.sharding import Mesh, PartitionSpec as P

DH = 128
SLAB = 16
TOKENS = 8192
HEADS = 64
TQ = 128
BK = 2048
ROWS = 1024
SLABS_HERE = ROWS // SLAB
FOLD = DH ** (-0.5) * 1.4426950408889634
AXES = ("x", "yl", "core", "zh", "zl", "yh")
HEAD_AXES = ("yl", "zh", "zl", "yh")


def split_kernel(q_ref, k_ref, v_ref, out_ref):
    for yl in range(4):
        for zh in range(2):
            for zl in range(4):
                for yh in range(2):
                    to = yl * 16 + zh * 8 + zl * 2 + yh
                    head = zl * 16 + yl * 4 + zh * 2 + yh
                    cols = slice(head * DH, (head + 1) * DH)
                    out_ref[to, 0:16, :] = q_ref[:, cols]
                    out_ref[to, 16:32, :] = k_ref[:, cols]
                    out_ref[to, 32:48, :] = v_ref[:, cols]


def split_heads(queries, keys, values):
    vmem = pl.BlockSpec(memory_space=pltpu.VMEM)
    return pl.pallas_call(
        split_kernel,
        out_shape=jax.ShapeDtypeStruct((HEADS, 48, DH), jnp.bfloat16),
        in_specs=[vmem, vmem, vmem],
        out_specs=vmem,
        name="split_heads",
    )(queries, keys, values)


def doc_start(positions, starts):
    first = jnp.zeros_like(positions)
    for start in starts:
        first = jnp.where(positions >= start, start, first)
    return first


def attend_kernel(slab_ref, dst_ref, start_ref, home_ref, *refs):
    shards, (out_ref, q_s, k_s, v_s, sem_q, sem_k, sem_v) = refs[:8], refs[8:]
    for i, shard in enumerate(shards):
        for yl in range(4):
            h = home_ref[i] + yl * 2
            for buf, lo, sem in ((q_s, 0, sem_q), (k_s, 16, sem_k), (v_s, 32, sem_v)):
                pltpu.make_async_copy(
                    shard.at[yl, :, pl.ds(lo, SLAB), :], buf.at[h], sem
                ).start()
    pltpu.make_async_copy(q_s, q_s, sem_q).wait()
    pltpu.make_async_copy(k_s, k_s, sem_k).wait()
    pltpu.make_async_copy(v_s, v_s, sem_v).wait()
    starts = [start_ref[i] for i in range(8)]
    per_tile = TQ // SLAB
    blocks = BK // 256

    def tile(t, carry):
        slabs = [slab_ref[t * per_tile + i] for i in range(per_tile)]
        q = jnp.concatenate([q_s[j >> 4, j & 15] for j in slabs], axis=0)
        row = lax.broadcasted_iota(jnp.int32, (SLAB, DH), 0)
        pos = jnp.concatenate([row + j * SLAB for j in slabs], axis=0)
        low = doc_start(pos, starts)
        last_pos = slabs[-1] * SLAB + SLAB - 1
        since = lax.broadcasted_iota(jnp.int32, (TQ, DH), 1) - low
        width = (pos - low).astype(jnp.uint32)
        low_first = doc_start(slabs[0] * SLAB, starts)
        begin = low_first >> 8
        count = (last_pos + 1 - begin * 256 + BK - 1) // BK
        begin = jnp.minimum(begin, 32 - count * blocks)
        base = begin * 256

        def block(i, state):
            high, denom, acc = state
            k = k_s[pl.ds(begin + i * blocks, blocks)].reshape(BK, DH)
            v = v_s[pl.ds(begin + i * blocks, blocks)].reshape(BK, DH)
            s = lax.dot_general(
                q, k, (((1,), (1,)), ((), ())), preferred_element_type=jnp.float32
            )
            gap = since + (base + i * BK)
            parts = []
            for m in range(BK // DH):
                ok = (gap + m * DH).astype(jnp.uint32) <= width
                parts.append(jnp.where(ok, s[:, m * DH:(m + 1) * DH], -1e30))
            top = parts[0]
            for part in parts[1:]:
                top = jnp.maximum(top, part)
            top = jnp.max(top, axis=1, keepdims=True) * FOLD
            new_high = jnp.maximum(high, jnp.broadcast_to(top, (TQ, DH)))
            scale = jnp.exp2(high - new_high)
            weights = [jnp.exp2(part * FOLD - new_high) for part in parts]
            denom = denom * scale
            for w in weights:
                denom = denom + w
            p = jnp.concatenate([w.astype(jnp.bfloat16) for w in weights], axis=1)
            acc = acc * scale + jnp.dot(p, v, preferred_element_type=jnp.float32)
            return new_high, denom, acc

        state = (
            jnp.full((TQ, DH), -1e30, jnp.float32),
            jnp.zeros((TQ, DH), jnp.float32),
            jnp.zeros((TQ, DH), jnp.float32),
        )
        high, denom, acc = lax.fori_loop(0, count, block, state)
        result = (acc / jnp.sum(denom, axis=1, keepdims=True)).astype(jnp.bfloat16)
        for i in range(per_tile):
            to = pl.multiple_of(dst_ref[t * per_tile + i], SLAB)
            out_ref[pl.ds(to, SLAB), :] = result[i * SLAB:(i + 1) * SLAB]
        return carry

    lax.fori_loop(0, ROWS // TQ, tile, 0)


def attend(slabs, dst, starts, homes, shards):
    smem = pl.BlockSpec(memory_space=pltpu.SMEM)
    shards = [shard.reshape(4, 16, 48, DH) for shard in shards]
    whole = pltpu.VMEM((32, 16, SLAB, DH), jnp.bfloat16)
    return pl.pallas_call(
        attend_kernel,
        out_shape=jax.ShapeDtypeStruct((ROWS, DH), jnp.bfloat16),
        in_specs=[smem] * 4 + [pl.BlockSpec(memory_space=pl.ANY)] * 8,
        out_specs=pl.BlockSpec(memory_space=pltpu.VMEM),
        scratch_shapes=[whole, whole, whole] + [pltpu.SemaphoreType.DMA] * 3,
        compiler_params=pltpu.CompilerParams(vmem_limit_bytes=32 * 1024 * 1024),
        cost_estimate=pl.CostEstimate(
            flops=2 * 10**9, bytes_accessed=8 * 2**20, transcendentals=2 * 10**6
        ),
        name="attend",
    )(slabs, dst, starts, homes, *shards)


def tables(doc_lengths, slab_owner):
    part = lax.axis_index("core") * 4 + lax.axis_index("x")
    yh = lax.axis_index("yh")
    n = slab_owner.shape[0]
    index = jnp.arange(n, dtype=jnp.int32)
    mine = (slab_owner >> 1) == part
    before = jnp.sum((mine[None, :] & (index[None, :] < index[:, None])).astype(jnp.int32), axis=1)
    here = jnp.arange(SLABS_HERE, dtype=jnp.int32)
    hit = mine[None, :] & (before[None, :] == here[:, None])
    slabs = jnp.sum(jnp.where(hit, index[None, :], 0), axis=1)
    low_owner = jnp.sum(jnp.where(hit, slab_owner[None, :] & 1, 0), axis=1)
    rank = jnp.sum(
        ((low_owner[None, :] == low_owner[:, None]) & (here[None, :] < here[:, None])).astype(jnp.int32),
        axis=1,
    )
    dst = (low_owner ^ yh) * 512 + rank * SLAB
    earlier = jnp.arange(8)[None, :] < jnp.arange(8)[:, None]
    starts = jnp.sum(jnp.where(earlier, doc_lengths[None, :], 0), axis=1)
    return slabs, dst, starts


def to_owner(swap):
    route = []
    for x in range(4):
        for core in range(2):
            for zh in range(2):
                for zl in range(4):
                    for yh in range(2):
                        source = (((x * 2 + core) * 2 + zh) * 4 + zl) * 2 + yh
                        target = (((zl * 2 + zh) * 2 + core) * 4 + x) * 2 + (yh ^ swap)
                        route.append((source, target))
    return route


def row_route(turn):
    route = []
    for x in range(4):
        for core in range(2):
            to_x, to_core = turn(x, core)
            route.append((x * 2 + core, (to_x % 4) * 2 + to_core))
    return route


def gather_row(mine):
    row = ("x", "core")
    ring = row_route(lambda x, core: (x + 1 - 2 * core, core))
    crossed = row_route(lambda x, core: (x - 1 + 2 * core, 1 - core))
    swap = row_route(lambda x, core: (x, 1 - core))
    near = lax.ppermute(mine, row, ring)
    near_other = lax.ppermute(mine, row, crossed)
    other = lax.ppermute(mine, row, swap)
    far = lax.ppermute(near, row, ring)
    back = lax.ppermute(near, row, swap)
    back_other = lax.ppermute(near_other, row, swap)
    far_other = lax.ppermute(far, row, swap)
    x, core = lax.axis_index("x"), lax.axis_index("core")
    behind = x - 1 + 2 * core
    ahead = x + 1 - 2 * core
    homes = jnp.stack(
        [
            (at & 3) * 8 + c
            for at, c in (
                (x, core),
                (x, 1 - core),
                (behind, core),
                (behind, 1 - core),
                (x + 2, core),
                (ahead, 1 - core),
                (ahead, core),
                (x + 2, 1 - core),
            )
        ]
    )
    return (mine, other, near, near_other, far, back, back_other, far_other), homes


def per_device(queries, keys, values, doc_lengths, slab_owner):
    slabs, dst, starts = tables(doc_lengths, slab_owner)
    parted = split_heads(queries, keys, values)
    landed = lax.all_to_all(parted, HEAD_AXES, split_axis=0, concat_axis=0, tiled=True)
    shards, homes = gather_row(landed)
    attended = attend(slabs, dst, starts, homes, shards)
    moved = ("x", "core", "zh", "zl", "yh")
    same = lax.ppermute(attended[:512], moved, to_owner(0))
    other = lax.ppermute(attended[512:], moved, to_owner(1))
    first = lax.axis_index("yh") == 0
    return jnp.concatenate(
        [jnp.where(first, same, other), jnp.where(first, other, same)], axis=1
    )


def solution(mesh):
    fine = Mesh(mesh.devices.reshape(4, 4, 2, 2, 4, 2), AXES)
    rows = P(AXES, None)
    return jax.shard_map(
        per_device,
        mesh=fine,
        in_specs=(rows, rows, rows, P(), P()),
        out_specs=P(("zh", "zl", "yh"), ("x", "yl", "core")),
        check_vma=False,
    )
```

```python
import jax
import jax.numpy as jnp
from jax import lax
from jax.experimental import pallas as pl
from jax.experimental.pallas import tpu as pltpu
from jax.sharding import Mesh, PartitionSpec as P

DH = 128
SLAB = 16
TOKENS = 8192
HEADS = 64
TQ = 128
BK = 2048
HALF = 1024
TOGETHER = 2
ROWS = 1024
SLABS_HERE = ROWS // SLAB
FOLD = DH ** (-0.5) * 1.4426950408889634
AXES = ("x", "yl", "core", "zh", "zl", "yh")
HEAD_AXES = ("yl", "zh", "zl", "yh")


def split_kernel(q_ref, k_ref, v_ref, out_ref):
    for yl in range(4):
        for zh in range(2):
            for zl in range(4):
                for yh in range(2):
                    to = yl * 16 + zh * 8 + zl * 2 + yh
                    head = zl * 16 + yl * 4 + zh * 2 + yh
                    cols = slice(head * DH, (head + 1) * DH)
                    out_ref[to, 0:16, :] = q_ref[:, cols]
                    out_ref[to, 16:32, :] = k_ref[:, cols]
                    out_ref[to, 32:48, :] = v_ref[:, cols]


def split_heads(queries, keys, values):
    vmem = pl.BlockSpec(memory_space=pltpu.VMEM)
    return pl.pallas_call(
        split_kernel,
        out_shape=jax.ShapeDtypeStruct((HEADS, 48, DH), jnp.bfloat16),
        in_specs=[vmem, vmem, vmem],
        out_specs=vmem,
        name="split_heads",
    )(queries, keys, values)


def doc_start(positions, starts):
    first = jnp.zeros_like(positions)
    for start in starts:
        first = jnp.where(positions >= start, start, first)
    return first


def attend_kernel(slab_ref, dst_ref, start_ref, home_ref, *refs):
    shards, (out_ref, q_s, k_s, v_s, sem_q, sem_k, sem_v) = refs[:8], refs[8:]
    for i, shard in enumerate(shards):
        for yl in range(4):
            h = home_ref[i] + yl * 2
            for buf, lo, sem in ((q_s, 0, sem_q), (k_s, 16, sem_k), (v_s, 32, sem_v)):
                pltpu.make_async_copy(
                    shard.at[yl, :, pl.ds(lo, SLAB), :], buf.at[h], sem
                ).start()
    pltpu.make_async_copy(q_s, q_s, sem_q).wait()
    pltpu.make_async_copy(k_s, k_s, sem_k).wait()
    pltpu.make_async_copy(v_s, v_s, sem_v).wait()
    starts = [start_ref[i] for i in range(8)]
    per_tile = TQ // SLAB
    blocks = BK // 256

    def setup(t):
        slabs = [slab_ref[t * per_tile + i] for i in range(per_tile)]
        q = jnp.concatenate([q_s[j >> 4, j & 15] for j in slabs], axis=0)
        row = lax.broadcasted_iota(jnp.int32, (SLAB, DH), 0)
        pos = jnp.concatenate([row + j * SLAB for j in slabs], axis=0)
        low = doc_start(pos, starts)
        since = lax.broadcasted_iota(jnp.int32, (TQ, DH), 1) - low
        width = (pos - low).astype(jnp.uint32)
        begin = doc_start(slabs[0] * SLAB, starts) >> 8
        end = slabs[-1] * SLAB + SLAB
        return q, since, width, begin, (end - begin * 256 + HALF - 1) // HALF

    def some(group, carry):
        tiles = [setup(group * TOGETHER + g) for g in range(TOGETHER)]
        count = tiles[0][4]
        for tile in tiles[1:]:
            count = jnp.maximum(count, tile[4])
        begins = [jnp.minimum(tile[3], 32 - count * (HALF // 256)) for tile in tiles]

        def block(start, size, states):
            some_blocks = size // 256
            scores = []
            for tile, begin in zip(tiles, begins):
                k = k_s[pl.ds(begin + start, some_blocks)].reshape(size, DH)
                scores.append(
                    lax.dot_general(
                        tile[0], k, (((1,), (1,)), ((), ())), preferred_element_type=jnp.float32
                    )
                )
            held = []
            for tile, begin, s, state in zip(tiles, begins, scores, states):
                high, denom, acc = state
                gap = tile[1] + (begin + start) * 256
                parts = []
                for m in range(size // DH):
                    ok = (gap + m * DH).astype(jnp.uint32) <= tile[2]
                    parts.append(jnp.where(ok, s[:, m * DH:(m + 1) * DH], -1e30))
                top = parts[0]
                for part in parts[1:]:
                    top = jnp.maximum(top, part)
                top = jnp.max(top, axis=1, keepdims=True) * FOLD
                new_high = jnp.maximum(high, jnp.broadcast_to(top, (TQ, DH)))
                scale = jnp.exp2(high - new_high)
                weights = [jnp.exp2(part * FOLD - new_high) for part in parts]
                denom = denom * scale
                for w in weights:
                    denom = denom + w
                p = jnp.concatenate([w.astype(jnp.bfloat16) for w in weights], axis=1)
                held.append((p, begin, scale, acc, new_high, denom))
            after = []
            for p, begin, scale, acc, new_high, denom in held:
                v = v_s[pl.ds(begin + start, some_blocks)].reshape(size, DH)
                acc = acc * scale + jnp.dot(p, v, preferred_element_type=jnp.float32)
                after.append((new_high, denom, acc))
            return after

        empty = (
            jnp.full((TQ, DH), -1e30, jnp.float32),
            jnp.zeros((TQ, DH), jnp.float32),
            jnp.zeros((TQ, DH), jnp.float32),
        )
        states = lax.fori_loop(
            0, count >> 1, lambda i, states: block(i * blocks, BK, states), [empty] * TOGETHER
        )
        states = lax.fori_loop(
            0, count & 1, lambda i, states: block((count >> 1) * blocks, HALF, states), states
        )
        for g, (high, denom, acc) in enumerate(states):
            result = (acc / jnp.sum(denom, axis=1, keepdims=True)).astype(jnp.bfloat16)
            for i in range(per_tile):
                to = dst_ref[(group * TOGETHER + g) * per_tile + i]
                out_ref[pl.ds(pl.multiple_of(to, SLAB), SLAB), :] = result[i * SLAB:(i + 1) * SLAB]
        return carry

    lax.fori_loop(0, ROWS // TQ // TOGETHER, some, 0)


def attend(slabs, dst, starts, homes, shards):
    smem = pl.BlockSpec(memory_space=pltpu.SMEM)
    shards = [shard.reshape(4, 16, 48, DH) for shard in shards]
    whole = pltpu.VMEM((32, 16, SLAB, DH), jnp.bfloat16)
    return pl.pallas_call(
        attend_kernel,
        out_shape=jax.ShapeDtypeStruct((ROWS, DH), jnp.bfloat16),
        in_specs=[smem] * 4 + [pl.BlockSpec(memory_space=pl.ANY)] * 8,
        out_specs=pl.BlockSpec(memory_space=pltpu.VMEM),
        scratch_shapes=[whole, whole, whole] + [pltpu.SemaphoreType.DMA] * 3,
        compiler_params=pltpu.CompilerParams(vmem_limit_bytes=32 * 1024 * 1024),
        cost_estimate=pl.CostEstimate(
            flops=2 * 10**9, bytes_accessed=8 * 2**20, transcendentals=2 * 10**6
        ),
        name="attend",
    )(slabs, dst, starts, homes, *shards)


def tables(doc_lengths, slab_owner):
    part = lax.axis_index("core") * 4 + lax.axis_index("x")
    yh = lax.axis_index("yh")
    n = slab_owner.shape[0]
    index = jnp.arange(n, dtype=jnp.int32)
    mine = (slab_owner >> 1) == part
    before = jnp.sum((mine[None, :] & (index[None, :] < index[:, None])).astype(jnp.int32), axis=1)
    here = jnp.arange(SLABS_HERE, dtype=jnp.int32)
    hit = mine[None, :] & (before[None, :] == here[:, None])
    slabs = jnp.sum(jnp.where(hit, index[None, :], 0), axis=1)
    low_owner = jnp.sum(jnp.where(hit, slab_owner[None, :] & 1, 0), axis=1)
    rank = jnp.sum(
        ((low_owner[None, :] == low_owner[:, None]) & (here[None, :] < here[:, None])).astype(jnp.int32),
        axis=1,
    )
    dst = (low_owner ^ yh) * 512 + rank * SLAB
    earlier = jnp.arange(8)[None, :] < jnp.arange(8)[:, None]
    starts = jnp.sum(jnp.where(earlier, doc_lengths[None, :], 0), axis=1)
    return slabs, dst, starts


def to_owner(swap):
    route = []
    for x in range(4):
        for core in range(2):
            for zh in range(2):
                for zl in range(4):
                    for yh in range(2):
                        source = (((x * 2 + core) * 2 + zh) * 4 + zl) * 2 + yh
                        target = (((zl * 2 + zh) * 2 + core) * 4 + x) * 2 + (yh ^ swap)
                        route.append((source, target))
    return route


def row_route(turn):
    route = []
    for x in range(4):
        for core in range(2):
            to_x, to_core = turn(x, core)
            route.append((x * 2 + core, (to_x % 4) * 2 + to_core))
    return route


def gather_row(mine):
    row = ("x", "core")
    ring = row_route(lambda x, core: (x + 1 - 2 * core, core))
    crossed = row_route(lambda x, core: (x - 1 + 2 * core, 1 - core))
    swap = row_route(lambda x, core: (x, 1 - core))
    near = lax.ppermute(mine, row, ring)
    near_other = lax.ppermute(mine, row, crossed)
    other = lax.ppermute(mine, row, swap)
    far = lax.ppermute(near, row, ring)
    back = lax.ppermute(near, row, swap)
    back_other = lax.ppermute(near_other, row, swap)
    far_other = lax.ppermute(far, row, swap)
    x, core = lax.axis_index("x"), lax.axis_index("core")
    behind = x - 1 + 2 * core
    ahead = x + 1 - 2 * core
    homes = jnp.stack(
        [
            (at & 3) * 8 + c
            for at, c in (
                (x, core),
                (x, 1 - core),
                (behind, core),
                (behind, 1 - core),
                (x + 2, core),
                (ahead, 1 - core),
                (ahead, core),
                (x + 2, 1 - core),
            )
        ]
    )
    return (mine, other, near, near_other, far, back, back_other, far_other), homes


def per_device(queries, keys, values, doc_lengths, slab_owner):
    slabs, dst, starts = tables(doc_lengths, slab_owner)
    parted = split_heads(queries, keys, values)
    landed = lax.all_to_all(parted, HEAD_AXES, split_axis=0, concat_axis=0, tiled=True)
    shards, homes = gather_row(landed)
    attended = attend(slabs, dst, starts, homes, shards)
    moved = ("x", "core", "zh", "zl", "yh")
    same = lax.ppermute(attended[:512], moved, to_owner(0))
    other = lax.ppermute(attended[512:], moved, to_owner(1))
    first = lax.axis_index("yh") == 0
    return jnp.concatenate(
        [jnp.where(first, same, other), jnp.where(first, other, same)], axis=1
    )


def solution(mesh):
    fine = Mesh(mesh.devices.reshape(4, 4, 2, 2, 4, 2), AXES)
    rows = P(AXES, None)
    return jax.shard_map(
        per_device,
        mesh=fine,
        in_specs=(rows, rows, rows, P(), P()),
        out_specs=P(("zh", "zl", "yh"), ("x", "yl", "core")),
        check_vma=False,
    )
```

```python
import jax
import jax.numpy as jnp
from jax import lax
from jax.experimental import pallas as pl
from jax.experimental.pallas import tpu as pltpu
from jax.sharding import Mesh, PartitionSpec as P

DH = 128
SLAB = 16
TOKENS = 8192
HEADS = 64
TQ = 128
BK = 2048
HALF = 1024
TOGETHER = 2
ROWS = 1024
SLABS_HERE = ROWS // SLAB
FOLD = DH ** (-0.5) * 1.4426950408889634
AXES = ("x", "yl", "core", "zh", "zl", "yh")
HEAD_AXES = ("yl", "zh", "zl", "yh")


def split_kernel(q_ref, k_ref, v_ref, out_ref):
    for yl in range(4):
        for zh in range(2):
            for zl in range(4):
                for yh in range(2):
                    to = yl * 16 + zh * 8 + zl * 2 + yh
                    head = zl * 16 + yl * 4 + zh * 2 + yh
                    cols = slice(head * DH, (head + 1) * DH)
                    out_ref[to, 0:16, :] = q_ref[:, cols]
                    out_ref[to, 16:32, :] = k_ref[:, cols]
                    out_ref[to, 32:48, :] = v_ref[:, cols]


def split_heads(queries, keys, values):
    vmem = pl.BlockSpec(memory_space=pltpu.VMEM)
    return pl.pallas_call(
        split_kernel,
        out_shape=jax.ShapeDtypeStruct((HEADS, 48, DH), jnp.bfloat16),
        in_specs=[vmem, vmem, vmem],
        out_specs=vmem,
        name="split_heads",
    )(queries, keys, values)


def doc_start(positions, starts):
    first = jnp.zeros_like(positions)
    for start in starts:
        first = jnp.where(positions >= start, start, first)
    return first


def attend_kernel(slab_ref, dst_ref, start_ref, home_ref, *refs):
    shards, (out_ref, q_s, k_s, v_s, sem_q, sem_k, sem_v) = refs[:8], refs[8:]
    for i, shard in enumerate(shards):
        x, core = home_ref[i] >> 3, home_ref[i] & 1
        for buf, lo, sem in ((q_s, 0, sem_q), (k_s, 16, sem_k), (v_s, 32, sem_v)):
            pltpu.make_async_copy(
                shard.at[:, :, pl.ds(lo, SLAB), :],
                buf.reshape(4, 4, 2, 16, SLAB, DH).at[x, :, core],
                sem,
            ).start()
    pltpu.make_async_copy(q_s, q_s, sem_q).wait()
    pltpu.make_async_copy(k_s, k_s, sem_k).wait()
    pltpu.make_async_copy(v_s, v_s, sem_v).wait()
    starts = [start_ref[i] for i in range(8)]
    per_tile = TQ // SLAB
    blocks = BK // 256

    def setup(t):
        slabs = [slab_ref[t * per_tile + i] for i in range(per_tile)]
        q = jnp.concatenate([q_s[j >> 4, j & 15] for j in slabs], axis=0)
        row = lax.broadcasted_iota(jnp.int32, (SLAB, DH), 0)
        pos = jnp.concatenate([row + j * SLAB for j in slabs], axis=0)
        low = doc_start(pos, starts)
        since = lax.broadcasted_iota(jnp.int32, (TQ, DH), 1) - low
        width = (pos - low).astype(jnp.uint32)
        begin = doc_start(slabs[0] * SLAB, starts) >> 8
        end = slabs[-1] * SLAB + SLAB
        return q, since, width, begin, (end - begin * 256 + HALF - 1) // HALF

    def some(group, carry):
        tiles = [setup(group * TOGETHER + g) for g in range(TOGETHER)]
        count = tiles[0][4]
        for tile in tiles[1:]:
            count = jnp.maximum(count, tile[4])
        begins = [jnp.minimum(tile[3], 32 - count * (HALF // 256)) for tile in tiles]

        def block(start, size, states):
            some_blocks = size // 256
            scores = []
            for tile, begin in zip(tiles, begins):
                k = k_s[pl.ds(begin + start, some_blocks)].reshape(size, DH)
                scores.append(
                    lax.dot_general(
                        tile[0], k, (((1,), (1,)), ((), ())), preferred_element_type=jnp.float32
                    )
                )
            held = []
            for tile, begin, s, state in zip(tiles, begins, scores, states):
                high, denom, acc = state
                gap = tile[1] + (begin + start) * 256
                parts = []
                for m in range(size // DH):
                    ok = (gap + m * DH).astype(jnp.uint32) <= tile[2]
                    parts.append(jnp.where(ok, s[:, m * DH:(m + 1) * DH], -1e30))
                top = parts[0]
                for part in parts[1:]:
                    top = jnp.maximum(top, part)
                top = jnp.max(top, axis=1, keepdims=True) * FOLD
                new_high = jnp.maximum(high, jnp.broadcast_to(top, (TQ, DH)))
                scale = jnp.exp2(high - new_high)
                weights = [jnp.exp2(part * FOLD - new_high) for part in parts]
                denom = denom * scale
                for w in weights:
                    denom = denom + w
                p = jnp.concatenate([w.astype(jnp.bfloat16) for w in weights], axis=1)
                held.append((p, begin, scale, acc, new_high, denom))
            after = []
            for p, begin, scale, acc, new_high, denom in held:
                v = v_s[pl.ds(begin + start, some_blocks)].reshape(size, DH)
                acc = acc * scale + jnp.dot(p, v, preferred_element_type=jnp.float32)
                after.append((new_high, denom, acc))
            return after

        empty = (
            jnp.full((TQ, DH), -1e30, jnp.float32),
            jnp.zeros((TQ, DH), jnp.float32),
            jnp.zeros((TQ, DH), jnp.float32),
        )
        states = lax.fori_loop(
            0, count >> 1, lambda i, states: block(i * blocks, BK, states), [empty] * TOGETHER
        )
        states = lax.fori_loop(
            0, count & 1, lambda i, states: block((count >> 1) * blocks, HALF, states), states
        )
        for g, (high, denom, acc) in enumerate(states):
            result = (acc / jnp.sum(denom, axis=1, keepdims=True)).astype(jnp.bfloat16)
            for i in range(per_tile):
                to = dst_ref[(group * TOGETHER + g) * per_tile + i]
                out_ref[pl.ds(pl.multiple_of(to, SLAB), SLAB), :] = result[i * SLAB:(i + 1) * SLAB]
        return carry

    lax.fori_loop(0, ROWS // TQ // TOGETHER, some, 0)


def attend(slabs, dst, starts, homes, shards):
    smem = pl.BlockSpec(memory_space=pltpu.SMEM)
    shards = [shard.reshape(4, 16, 48, DH) for shard in shards]
    whole = pltpu.VMEM((32, 16, SLAB, DH), jnp.bfloat16)
    return pl.pallas_call(
        attend_kernel,
        out_shape=jax.ShapeDtypeStruct((ROWS, DH), jnp.bfloat16),
        in_specs=[smem] * 4 + [pl.BlockSpec(memory_space=pl.ANY)] * 8,
        out_specs=pl.BlockSpec(memory_space=pltpu.VMEM),
        scratch_shapes=[whole, whole, whole] + [pltpu.SemaphoreType.DMA] * 3,
        compiler_params=pltpu.CompilerParams(vmem_limit_bytes=32 * 1024 * 1024),
        cost_estimate=pl.CostEstimate(
            flops=2 * 10**9, bytes_accessed=8 * 2**20, transcendentals=2 * 10**6
        ),
        name="attend",
    )(slabs, dst, starts, homes, *shards)


def tables(doc_lengths, slab_owner):
    part = lax.axis_index("core") * 4 + lax.axis_index("x")
    yh = lax.axis_index("yh")
    n = slab_owner.shape[0]
    index = jnp.arange(n, dtype=jnp.int32)
    mine = (slab_owner >> 1) == part
    before = jnp.sum((mine[None, :] & (index[None, :] < index[:, None])).astype(jnp.int32), axis=1)
    here = jnp.arange(SLABS_HERE, dtype=jnp.int32)
    hit = mine[None, :] & (before[None, :] == here[:, None])
    slabs = jnp.sum(jnp.where(hit, index[None, :], 0), axis=1)
    low_owner = jnp.sum(jnp.where(hit, slab_owner[None, :] & 1, 0), axis=1)
    rank = jnp.sum(
        ((low_owner[None, :] == low_owner[:, None]) & (here[None, :] < here[:, None])).astype(jnp.int32),
        axis=1,
    )
    dst = (low_owner ^ yh) * 512 + rank * SLAB
    earlier = jnp.arange(8)[None, :] < jnp.arange(8)[:, None]
    starts = jnp.sum(jnp.where(earlier, doc_lengths[None, :], 0), axis=1)
    return slabs, dst, starts


def to_owner(swap):
    route = []
    for x in range(4):
        for core in range(2):
            for zh in range(2):
                for zl in range(4):
                    for yh in range(2):
                        source = (((x * 2 + core) * 2 + zh) * 4 + zl) * 2 + yh
                        target = (((zl * 2 + zh) * 2 + core) * 4 + x) * 2 + (yh ^ swap)
                        route.append((source, target))
    return route


def row_route(turn):
    route = []
    for x in range(4):
        for core in range(2):
            to_x, to_core = turn(x, core)
            route.append((x * 2 + core, (to_x % 4) * 2 + to_core))
    return route


def gather_row(mine):
    row = ("x", "core")
    ring = row_route(lambda x, core: (x + 1 - 2 * core, core))
    crossed = row_route(lambda x, core: (x - 1 + 2 * core, 1 - core))
    swap = row_route(lambda x, core: (x, 1 - core))
    near = lax.ppermute(mine, row, ring)
    near_other = lax.ppermute(mine, row, crossed)
    other = lax.ppermute(mine, row, swap)
    far = lax.ppermute(near, row, ring)
    back = lax.ppermute(near, row, swap)
    back_other = lax.ppermute(near_other, row, swap)
    far_other = lax.ppermute(far, row, swap)
    x, core = lax.axis_index("x"), lax.axis_index("core")
    behind = x - 1 + 2 * core
    ahead = x + 1 - 2 * core
    homes = jnp.stack(
        [
            (at & 3) * 8 + c
            for at, c in (
                (x, core),
                (x, 1 - core),
                (behind, core),
                (behind, 1 - core),
                (x + 2, core),
                (ahead, 1 - core),
                (ahead, core),
                (x + 2, 1 - core),
            )
        ]
    )
    return (mine, other, near, near_other, far, back, back_other, far_other), homes


def per_device(queries, keys, values, doc_lengths, slab_owner):
    slabs, dst, starts = tables(doc_lengths, slab_owner)
    parted = split_heads(queries, keys, values)
    landed = lax.all_to_all(parted, HEAD_AXES, split_axis=0, concat_axis=0, tiled=True)
    shards, homes = gather_row(landed)
    attended = attend(slabs, dst, starts, homes, shards)
    moved = ("x", "core", "zh", "zl", "yh")
    same = lax.ppermute(attended[:512], moved, to_owner(0))
    other = lax.ppermute(attended[512:], moved, to_owner(1))
    first = lax.axis_index("yh") == 0
    return jnp.concatenate(
        [jnp.where(first, same, other), jnp.where(first, other, same)], axis=1
    )


def solution(mesh):
    fine = Mesh(mesh.devices.reshape(4, 4, 2, 2, 4, 2), AXES)
    rows = P(AXES, None)
    return jax.shard_map(
        per_device,
        mesh=fine,
        in_specs=(rows, rows, rows, P(), P()),
        out_specs=P(("zh", "zl", "yh"), ("x", "yl", "core")),
        check_vma=False,
    )
```

```python
import jax
import jax.numpy as jnp
from jax import lax
from jax.experimental import pallas as pl
from jax.experimental.pallas import tpu as pltpu
from jax.sharding import Mesh, PartitionSpec as P

DH = 128
SLAB = 16
TOKENS = 8192
HEADS = 64
TQ = 128
BK = 2048
HALF = 1024
TOGETHER = 2
ROWS = 512
SLABS_HERE = ROWS // SLAB
FOLD = DH ** (-0.5) * 1.4426950408889634
AXES = ("x", "yl", "core", "zh", "zl", "yh")
HEAD_AXES = ("yl", "zh", "zl", "yh")


def split_kernel(q_ref, k_ref, v_ref, out_ref):
    for yl in range(4):
        for zh in range(2):
            for zl in range(4):
                for yh in range(2):
                    to = yl * 16 + zh * 8 + zl * 2 + yh
                    head = zl * 16 + yl * 4 + zh * 2 + yh
                    cols = slice(head * DH, (head + 1) * DH)
                    out_ref[to, 0:16, :] = q_ref[:, cols]
                    out_ref[to, 16:32, :] = k_ref[:, cols]
                    out_ref[to, 32:48, :] = v_ref[:, cols]


def split_heads(queries, keys, values):
    vmem = pl.BlockSpec(memory_space=pltpu.VMEM)
    return pl.pallas_call(
        split_kernel,
        out_shape=jax.ShapeDtypeStruct((HEADS, 48, DH), jnp.bfloat16),
        in_specs=[vmem, vmem, vmem],
        out_specs=vmem,
        name="split_heads",
    )(queries, keys, values)


def doc_start(positions, starts):
    first = jnp.zeros_like(positions)
    for start in starts:
        first = jnp.where(positions >= start, start, first)
    return first


def attend_kernel(slab_ref, start_ref, home_ref, *refs):
    shards, (out_ref, q_s, k_s, v_s, sem_q, sem_k, sem_v) = refs[:8], refs[8:]
    for i, shard in enumerate(shards):
        x, core = home_ref[i] >> 3, home_ref[i] & 1
        for buf, lo, sem in ((q_s, 0, sem_q), (k_s, 16, sem_k), (v_s, 32, sem_v)):
            pltpu.make_async_copy(
                shard.at[:, :, pl.ds(lo, SLAB), :],
                buf.reshape(4, 4, 2, 16, SLAB, DH).at[x, :, core],
                sem,
            ).start()
    pltpu.make_async_copy(q_s, q_s, sem_q).wait()
    pltpu.make_async_copy(k_s, k_s, sem_k).wait()
    pltpu.make_async_copy(v_s, v_s, sem_v).wait()
    starts = [start_ref[i] for i in range(8)]
    per_tile = TQ // SLAB
    blocks = BK // 256

    def setup(t):
        slabs = [slab_ref[t * per_tile + i] for i in range(per_tile)]
        q = jnp.concatenate([q_s[j >> 4, j & 15] for j in slabs], axis=0)
        row = lax.broadcasted_iota(jnp.int32, (SLAB, DH), 0)
        pos = jnp.concatenate([row + j * SLAB for j in slabs], axis=0)
        low = doc_start(pos, starts)
        since = lax.broadcasted_iota(jnp.int32, (TQ, DH), 1) - low
        width = (pos - low).astype(jnp.uint32)
        begin = doc_start(slabs[0] * SLAB, starts) >> 8
        end = slabs[-1] * SLAB + SLAB
        return q, since, width, begin, (end - begin * 256 + HALF - 1) // HALF

    def some(group, carry):
        tiles = [setup(group * TOGETHER + g) for g in range(TOGETHER)]
        count = tiles[0][4]
        for tile in tiles[1:]:
            count = jnp.maximum(count, tile[4])
        begins = [jnp.minimum(tile[3], 32 - count * (HALF // 256)) for tile in tiles]

        def block(start, size, states):
            some_blocks = size // 256
            scores = []
            for tile, begin in zip(tiles, begins):
                k = k_s[pl.ds(begin + start, some_blocks)].reshape(size, DH)
                scores.append(
                    lax.dot_general(
                        tile[0], k, (((1,), (1,)), ((), ())), preferred_element_type=jnp.float32
                    )
                )
            held = []
            for tile, begin, s, state in zip(tiles, begins, scores, states):
                high, denom, acc = state
                gap = tile[1] + (begin + start) * 256
                parts = []
                for m in range(size // DH):
                    ok = (gap + m * DH).astype(jnp.uint32) <= tile[2]
                    parts.append(jnp.where(ok, s[:, m * DH:(m + 1) * DH], -1e30))
                top = parts[0]
                for part in parts[1:]:
                    top = jnp.maximum(top, part)
                top = jnp.max(top, axis=1, keepdims=True) * FOLD
                new_high = jnp.maximum(high, jnp.broadcast_to(top, (TQ, DH)))
                scale = jnp.exp2(high - new_high)
                weights = [jnp.exp2(part * FOLD - new_high) for part in parts]
                denom = denom * scale
                for w in weights:
                    denom = denom + w
                p = jnp.concatenate([w.astype(jnp.bfloat16) for w in weights], axis=1)
                held.append((p, begin, scale, acc, new_high, denom))
            after = []
            for p, begin, scale, acc, new_high, denom in held:
                v = v_s[pl.ds(begin + start, some_blocks)].reshape(size, DH)
                acc = acc * scale + jnp.dot(p, v, preferred_element_type=jnp.float32)
                after.append((new_high, denom, acc))
            return after

        empty = (
            jnp.full((TQ, DH), -1e30, jnp.float32),
            jnp.zeros((TQ, DH), jnp.float32),
            jnp.zeros((TQ, DH), jnp.float32),
        )
        states = lax.fori_loop(
            0, count >> 1, lambda i, states: block(i * blocks, BK, states), [empty] * TOGETHER
        )
        states = lax.fori_loop(
            0, count & 1, lambda i, states: block((count >> 1) * blocks, HALF, states), states
        )
        for g, (high, denom, acc) in enumerate(states):
            result = (acc / jnp.sum(denom, axis=1, keepdims=True)).astype(jnp.bfloat16)
            out_ref[pl.ds(pl.multiple_of((group * TOGETHER + g) * TQ, TQ), TQ), :] = result
        return carry

    if out_ref.shape[0] > ROWS:
        out_ref[ROWS:, :] = jnp.zeros((out_ref.shape[0] - ROWS, DH), jnp.bfloat16)
    lax.fori_loop(0, ROWS // TQ // TOGETHER, some, 0)


def attend(slabs, starts, homes, shards, extra):
    smem = pl.BlockSpec(memory_space=pltpu.SMEM)
    shards = [shard.reshape(4, 16, 48, DH) for shard in shards]
    whole = pltpu.VMEM((32, 16, SLAB, DH), jnp.bfloat16)
    return pl.pallas_call(
        attend_kernel,
        out_shape=jax.ShapeDtypeStruct((ROWS + extra, DH), jnp.bfloat16),
        in_specs=[smem] * 3 + [pl.BlockSpec(memory_space=pl.ANY)] * 8,
        out_specs=pl.BlockSpec(memory_space=pltpu.VMEM),
        scratch_shapes=[whole, whole, whole] + [pltpu.SemaphoreType.DMA] * 3,
        compiler_params=pltpu.CompilerParams(vmem_limit_bytes=32 * 1024 * 1024),
        cost_estimate=pl.CostEstimate(
            flops=2 * 10**9, bytes_accessed=8 * 2**20, transcendentals=2 * 10**6
        ),
        name="attend",
    )(slabs, starts, homes, *shards)


def tables(doc_lengths, slab_owner, flip):
    part = lax.axis_index("core") * 4 + lax.axis_index("x")
    owner = part * 2 + (lax.axis_index("yh") ^ flip)
    n = slab_owner.shape[0]
    index = jnp.arange(n, dtype=jnp.int32)
    mine = slab_owner == owner
    before = jnp.sum((mine[None, :] & (index[None, :] < index[:, None])).astype(jnp.int32), axis=1)
    here = jnp.arange(SLABS_HERE, dtype=jnp.int32)
    hit = mine[None, :] & (before[None, :] == here[:, None])
    slabs = jnp.sum(jnp.where(hit, index[None, :], 0), axis=1)
    earlier = jnp.arange(8)[None, :] < jnp.arange(8)[:, None]
    starts = jnp.sum(jnp.where(earlier, doc_lengths[None, :], 0), axis=1)
    return slabs, starts


def to_owner(swap):
    route = []
    for x in range(4):
        for core in range(2):
            for zh in range(2):
                for zl in range(4):
                    for yh in range(2):
                        source = (((x * 2 + core) * 2 + zh) * 4 + zl) * 2 + yh
                        target = (((zl * 2 + zh) * 2 + core) * 4 + x) * 2 + (yh ^ swap)
                        route.append((source, target))
    return route


def row_route(turn):
    route = []
    for x in range(4):
        for core in range(2):
            to_x, to_core = turn(x, core)
            route.append((x * 2 + core, (to_x % 4) * 2 + to_core))
    return route


def gather_row(mine):
    row = ("x", "core")
    ring = row_route(lambda x, core: (x + 1 - 2 * core, core))
    crossed = row_route(lambda x, core: (x - 1 + 2 * core, 1 - core))
    swap = row_route(lambda x, core: (x, 1 - core))
    near = lax.ppermute(mine, row, ring)
    near_other = lax.ppermute(mine, row, crossed)
    other = lax.ppermute(mine, row, swap)
    far = lax.ppermute(near, row, ring)
    back = lax.ppermute(near, row, swap)
    back_other = lax.ppermute(near_other, row, swap)
    far_other = lax.ppermute(far, row, swap)
    x, core = lax.axis_index("x"), lax.axis_index("core")
    behind = x - 1 + 2 * core
    ahead = x + 1 - 2 * core
    homes = jnp.stack(
        [
            (at & 3) * 8 + c
            for at, c in (
                (x, core),
                (x, 1 - core),
                (behind, core),
                (behind, 1 - core),
                (x + 2, core),
                (ahead, 1 - core),
                (ahead, core),
                (x + 2, 1 - core),
            )
        ]
    )
    return (mine, other, near, near_other, far, back, back_other, far_other), homes


def per_device(queries, keys, values, doc_lengths, slab_owner):
    far_slabs, starts = tables(doc_lengths, slab_owner, 1)
    near_slabs, _ = tables(doc_lengths, slab_owner, 0)
    parted = split_heads(queries, keys, values)
    landed = lax.all_to_all(parted, HEAD_AXES, split_axis=0, concat_axis=0, tiled=True)
    shards, homes = gather_row(landed)
    moved = ("x", "core", "zh", "zl", "yh")
    crossing = attend(far_slabs, starts, homes, shards, 16)
    other = lax.ppermute(crossing, moved, to_owner(1))[:512]
    staying = attend(near_slabs, starts, homes, shards, 0)
    same = lax.ppermute(staying, moved, to_owner(0))
    first = lax.axis_index("yh") == 0
    return jnp.concatenate(
        [jnp.where(first, same, other), jnp.where(first, other, same)], axis=1
    )


def solution(mesh):
    fine = Mesh(mesh.devices.reshape(4, 4, 2, 2, 4, 2), AXES)
    rows = P(AXES, None)
    return jax.shard_map(
        per_device,
        mesh=fine,
        in_specs=(rows, rows, rows, P(), P()),
        out_specs=P(("zh", "zl", "yh"), ("x", "yl", "core")),
        check_vma=False,
    )
```

```python
import jax
import jax.numpy as jnp
from jax import lax
from jax.experimental import pallas as pl
from jax.experimental.pallas import tpu as pltpu
from jax.sharding import Mesh, PartitionSpec as P

DH = 128
SLAB = 16
TOKENS = 8192
HEADS = 64
TQ = 128
BK = 2048
HALF = 1024
TOGETHER = 2
ROWS = 512
SLABS_HERE = ROWS // SLAB
FOLD = DH ** (-0.5) * 1.4426950408889634
AXES = ("x", "yl", "core", "zh", "zl", "yh")
HEAD_AXES = ("yl", "zh", "zl", "yh")


def split_kernel(q_ref, k_ref, v_ref, out_ref, in_s, out_s, in_sem, out_sem):
    width = HEADS * DH // 4
    loads = [
        pltpu.make_async_copy(
            ref.at[:, pl.ds(zl * width, width)], in_s.at[t, zl], in_sem.at[zl * 3 + t]
        )
        for zl in range(4)
        for t, ref in enumerate((q_ref, k_ref, v_ref))
    ]
    for load in loads:
        load.start()
    stores = []
    for zl in range(4):
        for t in range(3):
            loads[zl * 3 + t].wait()
        for n in range(16):
            yl, zh, yh = n >> 2, (n >> 1) & 1, n & 1
            for t in range(3):
                out_s[zl, yl, zh, yh, t * 16:(t + 1) * 16, :] = in_s[t, zl, :, n * DH:(n + 1) * DH]
        stores.append(pltpu.make_async_copy(out_s.at[zl], out_ref.at[:, :, zl], out_sem.at[zl]))
        stores[-1].start()
    for store in stores:
        store.wait()


def split_heads(queries, keys, values):
    hbm = pl.BlockSpec(memory_space=pl.ANY)
    return pl.pallas_call(
        split_kernel,
        out_shape=jax.ShapeDtypeStruct((4, 2, 4, 2, 48, DH), jnp.bfloat16),
        in_specs=[hbm, hbm, hbm],
        out_specs=hbm,
        scratch_shapes=[
            pltpu.VMEM((3, 4, SLAB, HEADS * DH // 4), jnp.bfloat16),
            pltpu.VMEM((4, 4, 2, 2, 48, DH), jnp.bfloat16),
            pltpu.SemaphoreType.DMA((12,)),
            pltpu.SemaphoreType.DMA((4,)),
        ],
        name="split_heads",
    )(queries, keys, values).reshape(HEADS, 48, DH)


def doc_start(positions, starts):
    first = jnp.zeros_like(positions)
    for start in starts:
        first = jnp.where(positions >= start, start, first)
    return first


def attend_kernel(slab_ref, start_ref, home_ref, *refs):
    shards, (out_ref, q_s, k_s, v_s, sem_q, sem_k, sem_v) = refs[:8], refs[8:]
    for i, shard in enumerate(shards):
        x, core = home_ref[i] >> 3, home_ref[i] & 1
        for buf, lo, sem in ((q_s, 0, sem_q), (k_s, 16, sem_k), (v_s, 32, sem_v)):
            pltpu.make_async_copy(
                shard.at[:, :, pl.ds(lo, SLAB), :],
                buf.reshape(4, 4, 2, 16, SLAB, DH).at[x, :, core],
                sem,
            ).start()
    pltpu.make_async_copy(q_s, q_s, sem_q).wait()
    pltpu.make_async_copy(k_s, k_s, sem_k).wait()
    pltpu.make_async_copy(v_s, v_s, sem_v).wait()
    starts = [start_ref[i] for i in range(8)]
    per_tile = TQ // SLAB
    blocks = BK // 256

    def setup(t):
        slabs = [slab_ref[t * per_tile + i] for i in range(per_tile)]
        q = jnp.concatenate([q_s[j >> 4, j & 15] for j in slabs], axis=0)
        row = lax.broadcasted_iota(jnp.int32, (SLAB, DH), 0)
        pos = jnp.concatenate([row + j * SLAB for j in slabs], axis=0)
        low = doc_start(pos, starts)
        since = lax.broadcasted_iota(jnp.int32, (TQ, DH), 1) - low
        width = (pos - low).astype(jnp.uint32)
        begin = doc_start(slabs[0] * SLAB, starts) >> 8
        end = slabs[-1] * SLAB + SLAB
        return q, since, width, begin, (end - begin * 256 + HALF - 1) // HALF

    def some(group, carry):
        tiles = [setup(group * TOGETHER + g) for g in range(TOGETHER)]
        count = tiles[0][4]
        for tile in tiles[1:]:
            count = jnp.maximum(count, tile[4])
        begins = [jnp.minimum(tile[3], 32 - count * (HALF // 256)) for tile in tiles]

        def block(start, size, states):
            some_blocks = size // 256
            scores = []
            for tile, begin in zip(tiles, begins):
                k = k_s[pl.ds(begin + start, some_blocks)].reshape(size, DH)
                scores.append(
                    lax.dot_general(
                        tile[0], k, (((1,), (1,)), ((), ())), preferred_element_type=jnp.float32
                    )
                )
            held = []
            for tile, begin, s, state in zip(tiles, begins, scores, states):
                high, denom, acc = state
                gap = tile[1] + (begin + start) * 256
                parts = []
                for m in range(size // DH):
                    ok = (gap + m * DH).astype(jnp.uint32) <= tile[2]
                    parts.append(jnp.where(ok, s[:, m * DH:(m + 1) * DH], -1e30))
                top = parts[0]
                for part in parts[1:]:
                    top = jnp.maximum(top, part)
                top = jnp.max(top, axis=1, keepdims=True) * FOLD
                new_high = jnp.maximum(high, jnp.broadcast_to(top, (TQ, DH)))
                scale = jnp.exp2(high - new_high)
                weights = [jnp.exp2(part * FOLD - new_high) for part in parts]
                denom = denom * scale
                for w in weights:
                    denom = denom + w
                p = jnp.concatenate([w.astype(jnp.bfloat16) for w in weights], axis=1)
                held.append((p, begin, scale, acc, new_high, denom))
            after = []
            for p, begin, scale, acc, new_high, denom in held:
                v = v_s[pl.ds(begin + start, some_blocks)].reshape(size, DH)
                acc = acc * scale + jnp.dot(p, v, preferred_element_type=jnp.float32)
                after.append((new_high, denom, acc))
            return after

        empty = (
            jnp.full((TQ, DH), -1e30, jnp.float32),
            jnp.zeros((TQ, DH), jnp.float32),
            jnp.zeros((TQ, DH), jnp.float32),
        )
        states = lax.fori_loop(
            0, count >> 1, lambda i, states: block(i * blocks, BK, states), [empty] * TOGETHER
        )
        states = lax.fori_loop(
            0, count & 1, lambda i, states: block((count >> 1) * blocks, HALF, states), states
        )
        for g, (high, denom, acc) in enumerate(states):
            result = (acc / jnp.sum(denom, axis=1, keepdims=True)).astype(jnp.bfloat16)
            out_ref[pl.ds(pl.multiple_of((group * TOGETHER + g) * TQ, TQ), TQ), :] = result
        return carry

    if out_ref.shape[0] > ROWS:
        out_ref[ROWS:, :] = jnp.zeros((out_ref.shape[0] - ROWS, DH), jnp.bfloat16)
    lax.fori_loop(0, ROWS // TQ // TOGETHER, some, 0)


def attend(slabs, starts, homes, shards, extra):
    smem = pl.BlockSpec(memory_space=pltpu.SMEM)
    shards = [shard.reshape(4, 16, 48, DH) for shard in shards]
    whole = pltpu.VMEM((32, 16, SLAB, DH), jnp.bfloat16)
    return pl.pallas_call(
        attend_kernel,
        out_shape=jax.ShapeDtypeStruct((ROWS + extra, DH), jnp.bfloat16),
        in_specs=[smem] * 3 + [pl.BlockSpec(memory_space=pl.ANY)] * 8,
        out_specs=pl.BlockSpec(memory_space=pltpu.VMEM),
        scratch_shapes=[whole, whole, whole] + [pltpu.SemaphoreType.DMA] * 3,
        compiler_params=pltpu.CompilerParams(vmem_limit_bytes=32 * 1024 * 1024),
        cost_estimate=pl.CostEstimate(
            flops=2 * 10**9, bytes_accessed=8 * 2**20, transcendentals=2 * 10**6
        ),
        name="attend",
    )(slabs, starts, homes, *shards)


def tables(doc_lengths, slab_owner, flip):
    part = lax.axis_index("core") * 4 + lax.axis_index("x")
    owner = part * 2 + (lax.axis_index("yh") ^ flip)
    n = slab_owner.shape[0]
    index = jnp.arange(n, dtype=jnp.int32)
    mine = slab_owner == owner
    before = jnp.sum((mine[None, :] & (index[None, :] < index[:, None])).astype(jnp.int32), axis=1)
    here = jnp.arange(SLABS_HERE, dtype=jnp.int32)
    hit = mine[None, :] & (before[None, :] == here[:, None])
    slabs = jnp.sum(jnp.where(hit, index[None, :], 0), axis=1)
    earlier = jnp.arange(8)[None, :] < jnp.arange(8)[:, None]
    starts = jnp.sum(jnp.where(earlier, doc_lengths[None, :], 0), axis=1)
    return slabs, starts


def to_owner(swap):
    route = []
    for x in range(4):
        for core in range(2):
            for zh in range(2):
                for zl in range(4):
                    for yh in range(2):
                        source = (((x * 2 + core) * 2 + zh) * 4 + zl) * 2 + yh
                        target = (((zl * 2 + zh) * 2 + core) * 4 + x) * 2 + (yh ^ swap)
                        route.append((source, target))
    return route


def row_route(turn):
    route = []
    for x in range(4):
        for core in range(2):
            to_x, to_core = turn(x, core)
            route.append((x * 2 + core, (to_x % 4) * 2 + to_core))
    return route


def gather_row(mine):
    row = ("x", "core")
    ring = row_route(lambda x, core: (x + 1 - 2 * core, core))
    crossed = row_route(lambda x, core: (x - 1 + 2 * core, 1 - core))
    swap = row_route(lambda x, core: (x, 1 - core))
    near = lax.ppermute(mine, row, ring)
    near_other = lax.ppermute(mine, row, crossed)
    other = lax.ppermute(mine, row, swap)
    far = lax.ppermute(near, row, ring)
    back = lax.ppermute(near, row, swap)
    back_other = lax.ppermute(near_other, row, swap)
    far_other = lax.ppermute(far, row, swap)
    x, core = lax.axis_index("x"), lax.axis_index("core")
    behind = x - 1 + 2 * core
    ahead = x + 1 - 2 * core
    homes = jnp.stack(
        [
            (at & 3) * 8 + c
            for at, c in (
                (x, core),
                (x, 1 - core),
                (behind, core),
                (behind, 1 - core),
                (x + 2, core),
                (ahead, 1 - core),
                (ahead, core),
                (x + 2, 1 - core),
            )
        ]
    )
    return (mine, other, near, near_other, far, back, back_other, far_other), homes


def per_device(queries, keys, values, doc_lengths, slab_owner):
    far_slabs, starts = tables(doc_lengths, slab_owner, 1)
    near_slabs, _ = tables(doc_lengths, slab_owner, 0)
    parted = split_heads(queries, keys, values)
    landed = lax.all_to_all(parted, HEAD_AXES, split_axis=0, concat_axis=0, tiled=True)
    shards, homes = gather_row(landed)
    moved = ("x", "core", "zh", "zl", "yh")
    crossing = attend(far_slabs, starts, homes, shards, 16)
    other = lax.ppermute(crossing, moved, to_owner(1))[:512]
    staying = attend(near_slabs, starts, homes, shards, 0)
    same = lax.ppermute(staying, moved, to_owner(0))
    first = lax.axis_index("yh") == 0
    return jnp.concatenate(
        [jnp.where(first, same, other), jnp.where(first, other, same)], axis=1
    )


def solution(mesh):
    fine = Mesh(mesh.devices.reshape(4, 4, 2, 2, 4, 2), AXES)
    rows = P(AXES, None)
    return jax.shard_map(
        per_device,
        mesh=fine,
        in_specs=(rows, rows, rows, P(), P()),
        out_specs=P(("zh", "zl", "yh"), ("x", "yl", "core")),
        check_vma=False,
    )
```
